32 devices in a mesh: seq: 4 (over x, core), view: 4 (over z), dp: 2 (over y).
Axes of the slice: x: 2, y: 2, z: 4, core: 2. Of those that a mesh axis runs over, the one named last changes fastest.
Arguments:
- latent: bfloat16 [8, 8, 64, 1152], P(('dp', 'view'), 'seq'), parts along dimension 0, may hold values from -6 to 6
- condition: bfloat16 [8, 8, 64, 1152], P(('dp', 'view'), 'seq'), parts along dimension 0, may hold values from -6 to 6
- cycle_order: int32 [8], P('dp'), parts along dimension 0, may hold values from 0 to 3, each once
- live_frames: int32 [8], P('dp'), parts along dimension 0, may hold values from 4 to 8
- w_qkv_ctrl: bfloat16 [1152, 3456], P('seq'), may hold values from -0.1875 to 0.1875
- w_out_ctrl: bfloat16 [1152, 1152], P('seq'), may hold values from -0.1875 to 0.1875
- w_join: bfloat16 [1152, 1152], P('seq'), may hold values from -0.1875 to 0.1875
- w_qkv_space: bfloat16 [1152, 3456], P('seq'), may hold values from -0.1875 to 0.1875
- w_out_space: bfloat16 [1152, 1152], P('seq'), may hold values from -0.1875 to 0.1875
- w_qkv_time: bfloat16 [1152, 3456], P('seq'), may hold values from -0.1875 to 0.1875
- w_out_time: bfloat16 [1152, 1152], P('seq'), may hold values from -0.1875 to 0.1875
- mod_ctrl: float32 [6, 1152], P('dp'), parts along dimension 0, may hold values from -3 to 3
- mod_space: float32 [6, 1152], P('dp'), parts along dimension 0, may hold values from -3 to 3
- mod_time: float32 [6, 1152], P('dp'), parts along dimension 0, may hold values from -3 to 3
- qk_gain: float32 [3, 2, 72], replicated, may hold values from 0.5 to 3.5, as said below
Outputs:
- result: bfloat16 [8, 8, 64, 1152], P(('dp', 'view'), None, 'seq'), parts along dimension 0
The draws below stay inside these ranges and needn't reach their ends.
There are 2 independent parts, one for each index of `dp`. The reference program is written for one: setup_inputs(seed, part) draws one part's arguments, and reference() takes and returns one part's arrays. A program takes and returns all parts, laid end to end along the dimension named above; an argument that names none is the same for every part. Nothing has to cross between parts.
Inputs may be any that keep to these rules, and one draw needn't show every extreme that they name: `cycle_order`: a permutation of the 4 cameras. `qk_gain`: positive gains.
All inputs are finite; a program needn't handle non-finite values.
Results may differ from the reference program's by a relative error of at most 0.01.
Values may be sent and summed in bfloat16 or wider, within the bound.
A program may use at most 192 MiB of HBM per device.

```python
import jax
import jax.numpy as jnp
from jax import lax

D = 1152
HEADS = 16
HEAD_DIM = 72
FRAMES = 8
PATCHES = 64
CAMS = 4


def draw_qk_gain(key, part):
    return jnp.exp(jax.random.uniform(key, (3, 2, HEAD_DIM), jnp.float32, jnp.log(0.5), jnp.log(2.0)))


def touch_ends(values, rng, low, top_value):
    longest = values.shape.index(max(values.shape))
    spots = []
    for shift in (0, 1):
        where = [jax.random.randint(jax.random.fold_in(rng, axis), (), 0, length) for axis, length in enumerate(values.shape)]
        where[longest] = (where[longest] + shift) % values.shape[longest]
        spots.append(tuple(where))
    return values.at[spots[0]].set(low).at[spots[1]].set(top_value)


def steps_of(key, dims, shards, low, largest):
    gain = 1.0
    for position, shards_of in shards:
        draws = jax.random.uniform(jax.random.fold_in(jax.random.fold_in(key, 6), position), (shards_of,), jnp.float32, low / len(shards), largest / len(shards))
        gain = gain * jnp.repeat(jnp.exp(draws), dims[position] // shards_of).reshape((-1,) + (1,) * (len(dims) - 1 - position))
    return gain


def normal_values(rng, extent, scale, bound, split=(), kind=jnp.bfloat16):
    array = jax.random.normal(rng, extent, jnp.float32) * scale
    if len(split) > 0:
        array = steps_of(rng, extent, split, -0.22, 0.18) * array
    return jnp.clip(array, min=-bound, max=bound).astype(kind)


def setup_inputs(seed: int = 0, part: int = 0) -> dict:
    arg_keys = jax.random.split(jax.random.key(seed), 16)
    part_splits = jax.random.split(jax.random.fold_in(arg_keys[15], part), 16)
    return {
        "latent": normal_values(part_splits[0], (CAMS, FRAMES, PATCHES, D), 1.0, 6.0, ((0, 4), (1, 4))),
        "condition": normal_values(part_splits[1], (CAMS, FRAMES, PATCHES, D), 1.0, 6.0, ((0, 4), (1, 4))),
        "cycle_order": jax.random.permutation(part_splits[2], CAMS).astype(jnp.int32),
        "live_frames": touch_ends(jax.random.randint(part_splits[3], (CAMS,), FRAMES // 2, FRAMES + 1), jax.random.fold_in(part_splits[3], 1), FRAMES // 2, FRAMES).astype(jnp.int32),
        "w_qkv_ctrl": normal_values(arg_keys[4], (D, 3 * D), D ** -0.5, 0.1875, ((0, 4),)),
        "w_out_ctrl": normal_values(arg_keys[5], (D, D), D ** -0.5, 0.1875, ((0, 4),)),
        "w_join": normal_values(arg_keys[6], (D, D), D ** -0.5, 0.1875, ((0, 4),)),
        "w_qkv_space": normal_values(arg_keys[7], (D, 3 * D), D ** -0.5, 0.1875, ((0, 4),)),
        "w_out_space": normal_values(arg_keys[8], (D, D), D ** -0.5, 0.1875, ((0, 4),)),
        "w_qkv_time": normal_values(arg_keys[9], (D, 3 * D), D ** -0.5, 0.1875, ((0, 4),)),
        "w_out_time": normal_values(arg_keys[10], (D, D), D ** -0.5, 0.1875, ((0, 4),)),
        "mod_ctrl": normal_values(part_splits[11], (3, D), 0.5, 3.0, (), jnp.float32),
        "mod_space": normal_values(part_splits[12], (3, D), 0.5, 3.0, (), jnp.float32),
        "mod_time": normal_values(part_splits[13], (3, D), 0.5, 3.0, (), jnp.float32),
        "qk_gain": draw_qk_gain(jax.random.fold_in(arg_keys[15], 71), part),
    }


epsilon = 1e-06
masked_score = -1e+30

def layer_norm(stream):
    average = lax.optimization_barrier(jnp.mean(stream, -1, keepdims=True))
    centred = stream - average
    spread = lax.optimization_barrier(jnp.mean(centred * centred, -1, keepdims=True))
    return centred * lax.rsqrt(spread + epsilon)

def modulate(stream, modulation):
    return (layer_norm(stream) * (1.0 + modulation[1]) + modulation[0]).astype(jnp.bfloat16)

def matmul(inputs, weight):
    in_shape = inputs.shape
    result = jnp.dot(inputs.reshape(-1, in_shape[-1]), weight, preferred_element_type=jnp.float32)
    return result.reshape(in_shape[:-1] + (weight.shape[1],))

def unit_rms(tensor):
    return tensor * lax.rsqrt(lax.optimization_barrier(jnp.mean(tensor * tensor, -1, keepdims=True)) + epsilon)

def split_heads(packed, gain_pair):
    width = packed.shape[-1] // 3
    head_size = width // HEADS
    pieces = packed.reshape(packed.shape[:-1] + (3, HEADS, head_size))
    queries = unit_rms(pieces[..., 0, :, :]) * gain_pair[0] * head_size ** (-0.5)
    key_rows = unit_rms(pieces[..., 1, :, :]) * gain_pair[1]
    value_rows = pieces[..., 2, :, :]
    return (queries.astype(jnp.bfloat16), key_rows.astype(jnp.bfloat16), value_rows.astype(jnp.bfloat16))

def attend(queries, key_rows, value_rows, allowed):
    scores = jnp.einsum('qhd,khd->hqk', queries.astype(jnp.float32), key_rows.astype(jnp.float32))
    scores = jnp.where(allowed[None, None, :], scores, masked_score)
    peak_value = lax.optimization_barrier(jnp.max(scores, -1, keepdims=True))
    terms = jnp.where(allowed[None, None, :], jnp.exp(scores - peak_value), 0.0)
    totals = lax.optimization_barrier(jnp.sum(terms, -1))
    weights = lax.optimization_barrier(terms.astype(jnp.bfloat16)).astype(jnp.float32)
    result = jnp.einsum('hqk,khd->qhd', weights, value_rows.astype(jnp.float32))
    return (result / totals.T[:, :, None]).astype(jnp.bfloat16)

def block(stream, modulation, gain_pair, w_qkv, w_out, attention_fn):
    normed = modulate(stream, modulation)
    queries, key_rows, value_rows = split_heads(matmul(normed, w_qkv), gain_pair)
    attended = attention_fn(queries, key_rows, value_rows)
    attended = attended.reshape(attended.shape[:-2] + (-1,))
    return stream + modulation[2] * matmul(attended, w_out)

def camera_mask(cycle_order):
    cameras = cycle_order.shape[0]
    onehot = (cycle_order[:, None] == jnp.arange(cameras, dtype=jnp.int32)[None, :]).astype(jnp.float32)
    after = jnp.roll(onehot, -1, axis=0)
    follow = jnp.dot(onehot.T, after)
    return follow + follow.T + jnp.eye(cameras, dtype=jnp.float32) > 0.5

def reference(latent, condition, cycle_order, live_frames, w_qkv_ctrl, w_out_ctrl, w_join, w_qkv_space, w_out_space, w_qkv_time, w_out_time, mod_ctrl, mod_space, mod_time, qk_gain):
    cameras, frames, patches, width = latent.shape
    base_stream = latent.astype(jnp.float32)
    ctrl_in = base_stream + condition.astype(jnp.float32)

    def own_frame(queries, key_rows, value_rows):
        head_shape = queries.shape[3:]
        flat = [tensor.reshape((cameras * frames, patches) + head_shape) for tensor in (queries, key_rows, value_rows)]
        every = jnp.ones((patches,), bool)
        result = lax.map(lambda triple: attend(triple[0], triple[1], triple[2], every), tuple(flat))
        return result.reshape(queries.shape)
    control = block(ctrl_in, mod_ctrl, qk_gain[0], w_qkv_ctrl, w_out_ctrl, own_frame).astype(jnp.bfloat16)
    joined = base_stream + matmul(control, w_join)
    allowed = camera_mask(cycle_order)

    def cross_view(queries, key_rows, value_rows):
        head_shape = queries.shape[3:]

        def single(block_index):
            camera = block_index // frames
            frame = block_index % frames
            key_all = key_rows[:, frame].reshape((cameras * patches,) + head_shape)
            value_all = value_rows[:, frame].reshape((cameras * patches,) + head_shape)
            mask_row = jnp.repeat(allowed[camera], patches)
            return attend(queries[camera, frame], key_all, value_all, mask_row)
        result = lax.map(single, jnp.arange(cameras * frames, dtype=jnp.int32))
        return result.reshape(queries.shape)
    spaced = block(joined, mod_space, qk_gain[1], w_qkv_space, w_out_space, cross_view).astype(jnp.bfloat16)
    frame_ok = jnp.arange(frames, dtype=jnp.int32)[None, :] < live_frames[:, None]

    def over_frames(queries, key_rows, value_rows):
        moved = [tensor.transpose(0, 2, 1, 3, 4) for tensor in (queries, key_rows, value_rows)]

        def per_camera(a, b, c, okay):
            return jax.vmap(lambda x, y, z: attend(x, y, z, okay))(a, b, c)
        inner = jax.vmap(per_camera)
        return inner(moved[0], moved[1], moved[2], frame_ok).transpose(0, 2, 1, 3, 4)
    result = block(spaced.astype(jnp.float32), mod_time, qk_gain[2], w_qkv_time, w_out_time, over_frames)
    return result.astype(jnp.bfloat16)
```

```python
import jax
import jax.numpy as jnp
from jax import lax
from jax.sharding import PartitionSpec as P

HEADS = 16

epsilon = 1e-06
masked_score = -1e30


def layer_norm(stream):
    average = jnp.mean(stream, -1, keepdims=True)
    centred = stream - average
    spread = jnp.mean(centred * centred, -1, keepdims=True)
    return centred * lax.rsqrt(spread + epsilon)


def modulate(stream, modulation):
    return (layer_norm(stream) * (1.0 + modulation[1]) + modulation[0]).astype(jnp.bfloat16)


def unit_rms(tensor):
    return tensor * lax.rsqrt(jnp.mean(tensor * tensor, -1, keepdims=True) + epsilon)


def swap_seq(array, bit, size):
    return lax.ppermute(array, "seq", [(i, i ^ bit) for i in range(size)])


def collect_rows(weight, seq_size, dp_size):
    rows, columns = weight.shape
    part = rows // dp_size
    seq, dp = lax.axis_index("seq"), lax.axis_index("dp")
    halves = weight.reshape(dp_size, part, columns)
    own_half = lax.dynamic_index_in_dim(halves, dp, 0, keepdims=False)
    pieces = [(weight, [(0, h) for h in range(dp_size)])]
    mine = [(own_half, 0)]
    bit = seq_size // 2
    while bit > 1:
        for array, mask in list(mine):
            got = swap_seq(array, bit, seq_size)
            mine.append((got, mask | bit))
            pieces.append((got, [(mask | bit, dp)]))
            for k in range(1, dp_size):
                other = lax.ppermute(got, "dp", [(i, (i + k) % dp_size) for i in range(dp_size)])
                pieces.append((other, [(mask | bit, (dp - k) % dp_size)]))
        bit //= 2
    if bit == 1:
        for array, places in list(pieces):
            got = swap_seq(array, 1, seq_size)
            pieces.append((got, [(mask | 1, h) for mask, h in places]))
    order = [jnp.bitwise_xor(seq, mask) * dp_size + h for _, places in pieces for mask, h in places]
    return jnp.concatenate([array for array, _ in pieces], axis=0), jnp.stack(order), part


def project(inputs, gathered):
    weight, order, part = gathered
    chunks = inputs.reshape(inputs.shape[0], -1, part)
    picked = jnp.take(chunks, order, axis=1, mode="clip").reshape(inputs.shape)
    return jnp.dot(picked, weight, preferred_element_type=jnp.float32)


def heads_of(packed, gain_pair, head_count):
    tokens = packed.shape[0]
    pieces = packed.reshape(tokens, 3, head_count, -1).transpose(1, 2, 0, 3)
    head_size = pieces.shape[-1]
    queries = unit_rms(pieces[0]) * gain_pair[0] * head_size ** (-0.5)
    keys = unit_rms(pieces[1]) * gain_pair[1]
    return queries.astype(jnp.bfloat16), keys.astype(jnp.bfloat16), pieces[2].astype(jnp.bfloat16)


def attend(queries, keys, values, allowed):
    scores = jnp.einsum("bqd,bkd->bqk", queries, keys, preferred_element_type=jnp.float32)
    if allowed is not None:
        scores = jnp.where(allowed[None], scores, masked_score)
    terms = jnp.exp(scores - jnp.max(scores, -1, keepdims=True))
    totals = jnp.sum(terms, -1, keepdims=True)
    mixed = jnp.einsum("bqk,bkd->bqd", terms.astype(jnp.bfloat16), values, preferred_element_type=jnp.float32)
    return (mixed / totals).astype(jnp.bfloat16)


def camera_mask(cycle_order):
    cameras = cycle_order.shape[0]
    onehot = (cycle_order[:, None] == jnp.arange(cameras, dtype=jnp.int32)[None, :]).astype(jnp.float32)
    after = jnp.roll(onehot, -1, axis=0)
    follow = jnp.dot(onehot.T, after)
    return follow + follow.T + jnp.eye(cameras, dtype=jnp.float32) > 0.5


def per_device(
    seq_size,
    view_size,
    dp_size,
    latent,
    condition,
    cycle_order,
    live_frames,
    w_qkv_ctrl,
    w_out_ctrl,
    w_join,
    w_qkv_space,
    w_out_space,
    w_qkv_time,
    w_out_time,
    mod_ctrl,
    mod_space,
    mod_time,
    qk_gain,
):
    frames_here, patches, width = latent.shape[1:]
    tokens = frames_here * patches
    head_size = width // HEADS
    view = lax.axis_index("view")
    view_heads = HEADS // view_size
    collect = lambda weight: collect_rows(weight, seq_size, dp_size)

    qkv_ctrl = collect(w_qkv_ctrl)
    out_ctrl = collect(w_out_ctrl)
    join = collect(w_join)
    columns = w_qkv_space.reshape(-1, 3, view_size, width // view_size)
    columns = lax.dynamic_index_in_dim(columns, view, 2, keepdims=False)
    qkv_space = collect(columns.reshape(-1, 3 * width // view_size))
    out_space = collect(w_out_space)
    qkv_time = collect(w_qkv_time)
    out_time = collect(w_out_time)

    base = latent.reshape(tokens, width).astype(jnp.float32)
    ctrl_in = base + condition.reshape(tokens, width).astype(jnp.float32)
    packed = project(modulate(ctrl_in, mod_ctrl), qkv_ctrl)
    parts = heads_of(packed, qk_gain[0], HEADS)
    by_frame = [part.reshape(HEADS * frames_here, patches, head_size) for part in parts]
    attended = attend(*by_frame, None).reshape(HEADS, tokens, head_size)
    flat = attended.transpose(1, 0, 2).reshape(tokens, width)
    control = (ctrl_in + mod_ctrl[2] * project(flat, out_ctrl)).astype(jnp.bfloat16)
    joined = base + project(control, join)

    normed = modulate(joined, mod_space)
    upward, downward = [normed], [normed]
    for _ in range(view_size - 1):
        upward.append(lax.ppermute(upward[-1], "view", [(i, i + 1) for i in range(view_size - 1)]))
        downward.append(lax.ppermute(downward[-1], "view", [(i + 1, i) for i in range(view_size - 1)]))
    everyone = [normed] + [jnp.where(view >= t, upward[t], downward[view_size - t]) for t in range(1, view_size)]
    cameras = (view - jnp.arange(view_size)) % view_size
    everyone = jnp.stack(everyone).reshape(view_size * tokens, width)
    packed = project(everyone, qkv_space)
    parts = heads_of(packed, qk_gain[1], view_heads)
    by_frame = [
        part.reshape(view_heads, view_size, frames_here, patches, head_size)
        .transpose(0, 2, 1, 3, 4)
        .reshape(view_heads * frames_here, view_size * patches, head_size)
        for part in parts
    ]
    near = camera_mask(cycle_order)[cameras][:, cameras]
    near = jnp.repeat(jnp.repeat(near, patches, 0), patches, 1)
    attended = attend(*by_frame, near).reshape(view_heads, frames_here, view_size, patches, head_size)
    attended = attended.transpose(2, 1, 3, 0, 4).reshape(view_size, tokens, width // view_size)
    attended = lax.all_to_all(attended[cameras], "view", split_axis=0, concat_axis=0, tiled=True)
    flat = attended.transpose(1, 0, 2).reshape(tokens, width)
    spaced = (joined + mod_space[2] * project(flat, out_space)).astype(jnp.bfloat16)

    spaced = spaced.reshape(1, frames_here, patches, width)
    patched = lax.all_to_all(spaced, "seq", split_axis=2, concat_axis=1, tiled=True)
    frames, patch_here = patched.shape[1:3]
    stream = patched.reshape(frames * patch_here, width).astype(jnp.float32)
    packed = project(modulate(stream, mod_time), qkv_time)
    parts = heads_of(packed, qk_gain[2], HEADS)
    own_live = lax.dynamic_index_in_dim(live_frames, view, 0, keepdims=False)
    place = jnp.arange(frames * patch_here, dtype=jnp.int32)
    same = place[:, None] % patch_here == place[None, :] % patch_here
    alive = place[None, :] // patch_here < own_live
    attended = attend(*parts, same & alive)
    flat = attended.transpose(1, 0, 2).reshape(frames * patch_here, width)
    result = stream + mod_time[2] * project(flat, out_time)
    return result.astype(jnp.bfloat16).reshape(patched.shape)


def solution(mesh):
    placed = (
        P(("dp", "view"), "seq", None, None),
        P(("dp", "view"), "seq", None, None),
        P("dp"),
        P("dp"),
        P("seq", None),
        P("seq", None),
        P("seq", None),
        P("seq", None),
        P("seq", None),
        P("seq", None),
        P("seq", None),
        P("dp", None),
        P("dp", None),
        P("dp", None),
        P(),
    )
    sizes = mesh.shape["seq"], mesh.shape["view"], mesh.shape["dp"]

    def run(*arrays):
        return per_device(*sizes, *arrays)

    return jax.shard_map(
        run,
        mesh=mesh,
        in_specs=placed,
        out_specs=P(("dp", "view"), None, "seq", None),
        check_vma=False,
    )
```

```python
import jax
import jax.numpy as jnp
from jax import lax
from jax.experimental import pallas as pl
from jax.experimental.pallas import tpu as pltpu
from jax.sharding import PartitionSpec as P

HEADS = 16

epsilon = 1e-06
masked_score = -1e30


def layer_norm(stream):
    average = jnp.mean(stream, -1, keepdims=True)
    centred = stream - average
    spread = jnp.mean(centred * centred, -1, keepdims=True)
    return centred * lax.rsqrt(spread + epsilon)


def modulate(stream, modulation):
    return (layer_norm(stream) * (1.0 + modulation[1]) + modulation[0]).astype(jnp.bfloat16)


def unit_rms(tensor):
    return tensor * lax.rsqrt(jnp.mean(tensor * tensor, -1, keepdims=True) + epsilon)


def collect_rows(weight, dp_size):
    rows, columns = weight.shape
    shares = weight.reshape(dp_size, rows // dp_size, columns)
    own_share = lax.dynamic_index_in_dim(shares, lax.axis_index("dp"), 0, keepdims=False)
    return lax.all_gather(own_share, ("seq", "dp"), axis=0, tiled=True)


def tile_of(size, unit, largest):
    tiles = [t for t in range(unit, min(size, largest) + 1, unit) if size % t == 0]
    return tiles[-1] if tiles else size


def matmul_kernel(x_ref, w_ref, out_ref):
    out_ref[...] = jnp.dot(x_ref[...], w_ref[...], preferred_element_type=jnp.float32)


def project(inputs, weight):
    rows, depth = inputs.shape
    columns = weight.shape[1]
    row_tile = tile_of(rows, 16, 1024)
    column_tile = tile_of(columns, 128, 512)
    return pl.pallas_call(
        matmul_kernel,
        grid=(rows // row_tile, columns // column_tile),
        in_specs=[
            pl.BlockSpec((row_tile, depth), lambda i, j: (i, 0)),
            pl.BlockSpec((depth, column_tile), lambda i, j: (0, j)),
        ],
        out_specs=pl.BlockSpec((row_tile, column_tile), lambda i, j: (i, j)),
        out_shape=jax.ShapeDtypeStruct((rows, columns), jnp.float32),
        compiler_params=pltpu.CompilerParams(vmem_limit_bytes=24 * 2**20),
        cost_estimate=pl.CostEstimate(
            flops=2 * rows * depth * columns,
            bytes_accessed=2 * (rows + columns) * depth + 4 * rows * columns,
            transcendentals=0,
        ),
    )(inputs, weight)


def heads_of(packed, gain_pair, head_count):
    tokens = packed.shape[0]
    pieces = packed.reshape(tokens, 3, head_count, -1).transpose(1, 2, 0, 3)
    head_size = pieces.shape[-1]
    queries = unit_rms(pieces[0]) * gain_pair[0] * head_size ** (-0.5)
    keys = unit_rms(pieces[1]) * gain_pair[1]
    return queries.astype(jnp.bfloat16), keys.astype(jnp.bfloat16), pieces[2].astype(jnp.bfloat16)


def attend(queries, keys, values, allowed):
    scores = jnp.einsum("bqd,bkd->bqk", queries, keys, preferred_element_type=jnp.float32)
    if allowed is not None:
        scores = jnp.where(allowed[None], scores, masked_score)
    terms = jnp.exp(scores - jnp.max(scores, -1, keepdims=True))
    totals = jnp.sum(terms, -1, keepdims=True)
    mixed = jnp.einsum("bqk,bkd->bqd", terms.astype(jnp.bfloat16), values, preferred_element_type=jnp.float32)
    return (mixed / totals).astype(jnp.bfloat16)


def camera_mask(cycle_order):
    cameras = cycle_order.shape[0]
    onehot = (cycle_order[:, None] == jnp.arange(cameras, dtype=jnp.int32)[None, :]).astype(jnp.float32)
    after = jnp.roll(onehot, -1, axis=0)
    follow = jnp.dot(onehot.T, after)
    return follow + follow.T + jnp.eye(cameras, dtype=jnp.float32) > 0.5


def per_device(
    view_size,
    dp_size,
    latent,
    condition,
    cycle_order,
    live_frames,
    w_qkv_ctrl,
    w_out_ctrl,
    w_join,
    w_qkv_space,
    w_out_space,
    w_qkv_time,
    w_out_time,
    mod_ctrl,
    mod_space,
    mod_time,
    qk_gain,
):
    frames_here, patches, width = latent.shape[1:]
    tokens = frames_here * patches
    head_size = width // HEADS
    view = lax.axis_index("view")
    view_heads = HEADS // view_size
    collect = lambda weight: collect_rows(weight, dp_size)

    qkv_ctrl = collect(w_qkv_ctrl)
    out_ctrl = collect(w_out_ctrl)
    join = collect(w_join)
    columns = w_qkv_space.reshape(-1, 3, view_size, width // view_size)
    columns = lax.dynamic_index_in_dim(columns, view, 2, keepdims=False)
    qkv_space = collect(columns.reshape(-1, 3 * width // view_size))
    out_space = collect(w_out_space)
    qkv_time = collect(w_qkv_time)
    out_time = collect(w_out_time)

    base = latent.reshape(tokens, width).astype(jnp.float32)
    ctrl_in = base + condition.reshape(tokens, width).astype(jnp.float32)
    packed = project(modulate(ctrl_in, mod_ctrl), qkv_ctrl)
    parts = heads_of(packed, qk_gain[0], HEADS)
    by_frame = [part.reshape(HEADS * frames_here, patches, head_size) for part in parts]
    attended = attend(*by_frame, None).reshape(HEADS, tokens, head_size)
    flat = attended.transpose(1, 0, 2).reshape(tokens, width)
    control = (ctrl_in + mod_ctrl[2] * project(flat, out_ctrl)).astype(jnp.bfloat16)
    joined = base + project(control, join)

    normed = modulate(joined, mod_space)
    upward, downward = [normed], [normed]
    for _ in range(view_size - 1):
        upward.append(lax.ppermute(upward[-1], "view", [(i, i + 1) for i in range(view_size - 1)]))
        downward.append(lax.ppermute(downward[-1], "view", [(i + 1, i) for i in range(view_size - 1)]))
    everyone = [normed] + [jnp.where(view >= t, upward[t], downward[view_size - t]) for t in range(1, view_size)]
    cameras = (view - jnp.arange(view_size)) % view_size
    everyone = jnp.stack(everyone).reshape(view_size * tokens, width)
    packed = project(everyone, qkv_space)
    parts = heads_of(packed, qk_gain[1], view_heads)
    by_frame = [
        part.reshape(view_heads, view_size, frames_here, patches, head_size)
        .transpose(0, 2, 1, 3, 4)
        .reshape(view_heads * frames_here, view_size * patches, head_size)
        for part in parts
    ]
    near = camera_mask(cycle_order)[cameras][:, cameras]
    near = jnp.repeat(jnp.repeat(near, patches, 0), patches, 1)
    attended = attend(*by_frame, near).reshape(view_heads, frames_here, view_size, patches, head_size)
    attended = attended.transpose(2, 1, 3, 0, 4).reshape(view_size, tokens, width // view_size)
    attended = lax.all_to_all(attended[cameras], "view", split_axis=0, concat_axis=0, tiled=True)
    flat = attended.transpose(1, 0, 2).reshape(tokens, width)
    spaced = (joined + mod_space[2] * project(flat, out_space)).astype(jnp.bfloat16)

    spaced = spaced.reshape(1, frames_here, patches, width)
    patched = lax.all_to_all(spaced, "seq", split_axis=2, concat_axis=1, tiled=True)
    frames, patch_here = patched.shape[1:3]
    stream = patched.reshape(frames * patch_here, width).astype(jnp.float32)
    packed = project(modulate(stream, mod_time), qkv_time)
    parts = heads_of(packed, qk_gain[2], HEADS)
    own_live = lax.dynamic_index_in_dim(live_frames, view, 0, keepdims=False)
    place = jnp.arange(frames * patch_here, dtype=jnp.int32)
    same = place[:, None] % patch_here == place[None, :] % patch_here
    alive = place[None, :] // patch_here < own_live
    attended = attend(*parts, same & alive)
    flat = attended.transpose(1, 0, 2).reshape(frames * patch_here, width)
    result = stream + mod_time[2] * project(flat, out_time)
    return result.astype(jnp.bfloat16).reshape(patched.shape)


def solution(mesh):
    placed = (
        P(("dp", "view"), "seq", None, None),
        P(("dp", "view"), "seq", None, None),
        P("dp"),
        P("dp"),
        P("seq", None),
        P("seq", None),
        P("seq", None),
        P("seq", None),
        P("seq", None),
        P("seq", None),
        P("seq", None),
        P("dp", None),
        P("dp", None),
        P("dp", None),
        P(),
    )
    sizes = mesh.shape["view"], mesh.shape["dp"]

    def run(*arrays):
        return per_device(*sizes, *arrays)

    return jax.shard_map(
        run,
        mesh=mesh,
        in_specs=placed,
        out_specs=P(("dp", "view"), None, "seq", None),
        check_vma=False,
    )
```

```python
import math

import jax
import jax.numpy as jnp
from jax import lax
from jax.experimental import pallas as pl
from jax.experimental.pallas import tpu as pltpu
from jax.sharding import PartitionSpec as P

HEADS = 16

epsilon = 1e-06
masked_score = -1e30


def layer_norm(stream):
    average = jnp.mean(stream, -1, keepdims=True)
    centred = stream - average
    spread = jnp.mean(centred * centred, -1, keepdims=True)
    return centred * lax.rsqrt(spread + epsilon)


def modulate(stream, modulation):
    return (layer_norm(stream) * (1.0 + modulation[1]) + modulation[0]).astype(jnp.bfloat16)


def unit_rms(tensor):
    return tensor * lax.rsqrt(jnp.mean(tensor * tensor, -1, keepdims=True) + epsilon)


def collect_rows(weight, dp_size):
    rows, columns = weight.shape
    shares = weight.reshape(dp_size, rows // dp_size, columns)
    own_share = lax.dynamic_index_in_dim(shares, lax.axis_index("dp"), 0, keepdims=False)
    return lax.all_gather(own_share, ("seq", "dp"), axis=0, tiled=True)


def pass_rows(weight, seq_size):
    pieces = [weight]
    for k in range(1, seq_size):
        pieces.append(lax.ppermute(weight, "seq", [(i, (i + k) % seq_size) for i in range(seq_size)]))
    order = (lax.axis_index("seq") - jnp.arange(seq_size)) % seq_size
    return jnp.concatenate(pieces, axis=0), order


def project_passed(inputs, passed):
    weight, order = passed
    chunks = inputs.reshape(inputs.shape[0], order.shape[0], -1)
    return project(jnp.take(chunks, order, axis=1, mode="clip").reshape(inputs.shape), weight)


def tile_of(size, unit, largest):
    tiles = [t for t in range(unit, min(size, largest) + 1, unit) if size % t == 0]
    return tiles[-1] if tiles else size


def matmul_kernel(x_ref, w_ref, out_ref):
    out_ref[...] = jnp.dot(x_ref[...], w_ref[...], preferred_element_type=jnp.float32)


def project(inputs, weight, first=0, columns=None):
    rows, depth = inputs.shape
    columns = columns or weight.shape[1]
    row_tile = tile_of(rows, 16, 1024)
    column_tile = tile_of(math.gcd(columns, first), 128, 512)
    skipped = first // column_tile
    return pl.pallas_call(
        matmul_kernel,
        grid=(rows // row_tile, columns // column_tile),
        in_specs=[
            pl.BlockSpec((row_tile, depth), lambda i, j: (i, 0)),
            pl.BlockSpec((depth, column_tile), lambda i, j: (0, j + skipped)),
        ],
        out_specs=pl.BlockSpec((row_tile, column_tile), lambda i, j: (i, j)),
        out_shape=jax.ShapeDtypeStruct((rows, columns), jnp.float32),
        compiler_params=pltpu.CompilerParams(vmem_limit_bytes=24 * 2**20),
        cost_estimate=pl.CostEstimate(
            flops=2 * rows * depth * columns,
            bytes_accessed=2 * (rows + columns) * depth + 4 * rows * columns,
            transcendentals=0,
        ),
    )(inputs, weight)


def heads_of(packed, gain_pair, head_count):
    tokens = packed.shape[0]
    pieces = packed.reshape(tokens, 3, head_count, -1).transpose(1, 2, 0, 3)
    head_size = pieces.shape[-1]
    queries = unit_rms(pieces[0]) * gain_pair[0] * head_size ** (-0.5)
    keys = unit_rms(pieces[1]) * gain_pair[1]
    return queries.astype(jnp.bfloat16), keys.astype(jnp.bfloat16), pieces[2].astype(jnp.bfloat16)


def attend(queries, keys, values, allowed):
    scores = jnp.einsum("bqd,bkd->bqk", queries, keys, preferred_element_type=jnp.float32)
    if allowed is not None:
        scores = jnp.where(allowed[None], scores, masked_score)
    terms = jnp.exp(scores - jnp.max(scores, -1, keepdims=True))
    totals = jnp.sum(terms, -1, keepdims=True)
    mixed = jnp.einsum("bqk,bkd->bqd", terms.astype(jnp.bfloat16), values, preferred_element_type=jnp.float32)
    return (mixed / totals).astype(jnp.bfloat16)


def camera_mask(cycle_order):
    cameras = cycle_order.shape[0]
    onehot = (cycle_order[:, None] == jnp.arange(cameras, dtype=jnp.int32)[None, :]).astype(jnp.float32)
    after = jnp.roll(onehot, -1, axis=0)
    follow = jnp.dot(onehot.T, after)
    return follow + follow.T + jnp.eye(cameras, dtype=jnp.float32) > 0.5


def per_device(
    seq_size,
    view_size,
    dp_size,
    latent,
    condition,
    cycle_order,
    live_frames,
    w_qkv_ctrl,
    w_out_ctrl,
    w_join,
    w_qkv_space,
    w_out_space,
    w_qkv_time,
    w_out_time,
    mod_ctrl,
    mod_space,
    mod_time,
    qk_gain,
):
    frames_here, patches, width = latent.shape[1:]
    tokens = frames_here * patches
    head_size = width // HEADS
    view = lax.axis_index("view")
    view_heads = HEADS // view_size
    collect = lambda weight: collect_rows(weight, dp_size)

    out_ctrl = pass_rows(w_out_ctrl, seq_size)
    join = pass_rows(w_join, seq_size)
    qkv_ctrl = collect(w_qkv_ctrl)
    columns = w_qkv_space.reshape(-1, 3, view_size, width // view_size)
    columns = lax.dynamic_index_in_dim(columns, view, 2, keepdims=False)
    space = collect(jnp.concatenate([w_out_space, columns.reshape(-1, 3 * width // view_size)], axis=1))
    time = collect(jnp.concatenate([w_qkv_time, w_out_time], axis=1))

    base = latent.reshape(tokens, width).astype(jnp.float32)
    ctrl_in = base + condition.reshape(tokens, width).astype(jnp.float32)
    packed = project(modulate(ctrl_in, mod_ctrl), qkv_ctrl)
    parts = heads_of(packed, qk_gain[0], HEADS)
    by_frame = [part.reshape(HEADS * frames_here, patches, head_size) for part in parts]
    attended = attend(*by_frame, None).reshape(HEADS, tokens, head_size)
    flat = attended.transpose(1, 0, 2).reshape(tokens, width)
    control = (ctrl_in + mod_ctrl[2] * project_passed(flat, out_ctrl)).astype(jnp.bfloat16)
    joined = base + project_passed(control, join)

    normed = modulate(joined, mod_space)
    upward, downward = [normed], [normed]
    for _ in range(view_size - 1):
        upward.append(lax.ppermute(upward[-1], "view", [(i, i + 1) for i in range(view_size - 1)]))
        downward.append(lax.ppermute(downward[-1], "view", [(i + 1, i) for i in range(view_size - 1)]))
    everyone = [normed] + [jnp.where(view >= t, upward[t], downward[view_size - t]) for t in range(1, view_size)]
    cameras = (view - jnp.arange(view_size)) % view_size
    everyone = jnp.stack(everyone).reshape(view_size * tokens, width)
    packed = project(everyone, space[:, width:])
    parts = heads_of(packed, qk_gain[1], view_heads)
    by_frame = [
        part.reshape(view_heads, view_size, frames_here, patches, head_size)
        .transpose(0, 2, 1, 3, 4)
        .reshape(view_heads * frames_here, view_size * patches, head_size)
        for part in parts
    ]
    near = camera_mask(cycle_order)[cameras][:, cameras]
    near = jnp.repeat(jnp.repeat(near, patches, 0), patches, 1)
    attended = attend(*by_frame, near).reshape(view_heads, frames_here, view_size, patches, head_size)
    attended = attended.transpose(2, 1, 3, 0, 4).reshape(view_size, tokens, width // view_size)
    attended = lax.all_to_all(attended[cameras], "view", split_axis=0, concat_axis=0, tiled=True)
    flat = attended.transpose(1, 0, 2).reshape(tokens, width)
    spaced = (joined + mod_space[2] * project(flat, space, 0, width)).astype(jnp.bfloat16)

    spaced = spaced.reshape(1, frames_here, patches, width)
    patched = lax.all_to_all(spaced, "seq", split_axis=2, concat_axis=1, tiled=True)
    frames, patch_here = patched.shape[1:3]
    stream = patched.reshape(frames * patch_here, width).astype(jnp.float32)
    packed = project(modulate(stream, mod_time), time, 0, 3 * width)
    parts = heads_of(packed, qk_gain[2], HEADS)
    own_live = lax.dynamic_index_in_dim(live_frames, view, 0, keepdims=False)
    place = jnp.arange(frames * patch_here, dtype=jnp.int32)
    same = place[:, None] % patch_here == place[None, :] % patch_here
    alive = place[None, :] // patch_here < own_live
    attended = attend(*parts, same & alive)
    flat = attended.transpose(1, 0, 2).reshape(frames * patch_here, width)
    result = stream + mod_time[2] * project(flat, time, 3 * width, width)
    return result.astype(jnp.bfloat16).reshape(patched.shape)


def solution(mesh):
    placed = (
        P(("dp", "view"), "seq", None, None),
        P(("dp", "view"), "seq", None, None),
        P("dp"),
        P("dp"),
        P("seq", None),
        P("seq", None),
        P("seq", None),
        P("seq", None),
        P("seq", None),
        P("seq", None),
        P("seq", None),
        P("dp", None),
        P("dp", None),
        P("dp", None),
        P(),
    )
    sizes = mesh.shape["seq"], mesh.shape["view"], mesh.shape["dp"]

    def run(*arrays):
        return per_device(*sizes, *arrays)

    return jax.shard_map(
        run,
        mesh=mesh,
        in_specs=placed,
        out_specs=P(("dp", "view"), None, "seq", None),
        check_vma=False,
    )
```

```python
import math

import jax
import jax.numpy as jnp
from jax import lax
from jax.experimental import pallas as pl
from jax.experimental.pallas import tpu as pltpu
from jax.sharding import PartitionSpec as P

HEADS = 16

epsilon = 1e-06
masked_score = -1e30


def layer_norm(stream):
    average = jnp.mean(stream, -1, keepdims=True)
    centred = stream - average
    spread = jnp.mean(centred * centred, -1, keepdims=True)
    return centred * lax.rsqrt(spread + epsilon)


def modulate(stream, modulation):
    return (layer_norm(stream) * (1.0 + modulation[1]) + modulation[0]).astype(jnp.bfloat16)


def unit_rms(tensor):
    return tensor * lax.rsqrt(jnp.mean(tensor * tensor, -1, keepdims=True) + epsilon)


def collect_rows(weight, dp_size):
    rows, columns = weight.shape
    shares = weight.reshape(dp_size, rows // dp_size, columns)
    own_share = lax.dynamic_index_in_dim(shares, lax.axis_index("dp"), 0, keepdims=False)
    return lax.all_gather(own_share, ("seq", "dp"), axis=0, tiled=True)


def tile_of(size, unit, largest):
    tiles = [t for t in range(unit, min(size, largest) + 1, unit) if size % t == 0]
    return tiles[-1] if tiles else size


def matmul_kernel(x_ref, w_ref, out_ref):
    out_ref[...] = jnp.dot(x_ref[...], w_ref[...], preferred_element_type=jnp.float32)


def project(inputs, weight, first=0, columns=None):
    rows, depth = inputs.shape
    columns = columns or weight.shape[1]
    row_tile = tile_of(rows, 16, 1024)
    column_tile = tile_of(math.gcd(columns, first), 128, 512)
    skipped = first // column_tile
    return pl.pallas_call(
        matmul_kernel,
        grid=(rows // row_tile, columns // column_tile),
        in_specs=[
            pl.BlockSpec((row_tile, depth), lambda i, j: (i, 0)),
            pl.BlockSpec((depth, column_tile), lambda i, j: (0, j + skipped)),
        ],
        out_specs=pl.BlockSpec((row_tile, column_tile), lambda i, j: (i, j)),
        out_shape=jax.ShapeDtypeStruct((rows, columns), jnp.float32),
        compiler_params=pltpu.CompilerParams(vmem_limit_bytes=24 * 2**20),
        cost_estimate=pl.CostEstimate(
            flops=2 * rows * depth * columns,
            bytes_accessed=2 * (rows + columns) * depth + 4 * rows * columns,
            transcendentals=0,
        ),
    )(inputs, weight)


def heads_of(packed, gain_pair, head_count):
    tokens = packed.shape[0]
    pieces = packed.reshape(tokens, 3, head_count, -1).transpose(1, 2, 0, 3)
    head_size = pieces.shape[-1]
    queries = unit_rms(pieces[0]) * gain_pair[0] * head_size ** (-0.5)
    keys = unit_rms(pieces[1]) * gain_pair[1]
    return queries.astype(jnp.bfloat16), keys.astype(jnp.bfloat16), pieces[2].astype(jnp.bfloat16)


def attend(queries, keys, values, allowed):
    scores = jnp.einsum("bqd,bkd->bqk", queries, keys, preferred_element_type=jnp.float32)
    if allowed is not None:
        scores = jnp.where(allowed[None], scores, masked_score)
    terms = jnp.exp(scores - jnp.max(scores, -1, keepdims=True))
    totals = jnp.sum(terms, -1, keepdims=True)
    mixed = jnp.einsum("bqk,bkd->bqd", terms.astype(jnp.bfloat16), values, preferred_element_type=jnp.float32)
    return (mixed / totals).astype(jnp.bfloat16)


def camera_mask(cycle_order):
    cameras = cycle_order.shape[0]
    onehot = (cycle_order[:, None] == jnp.arange(cameras, dtype=jnp.int32)[None, :]).astype(jnp.float32)
    after = jnp.roll(onehot, -1, axis=0)
    follow = jnp.dot(onehot.T, after)
    return follow + follow.T + jnp.eye(cameras, dtype=jnp.float32) > 0.5


def per_device(
    view_size,
    dp_size,
    latent,
    condition,
    cycle_order,
    live_frames,
    w_qkv_ctrl,
    w_out_ctrl,
    w_join,
    w_qkv_space,
    w_out_space,
    w_qkv_time,
    w_out_time,
    mod_ctrl,
    mod_space,
    mod_time,
    qk_gain,
):
    frames_here, patches, width = latent.shape[1:]
    tokens = frames_here * patches
    head_size = width // HEADS
    view = lax.axis_index("view")
    view_heads = HEADS // view_size
    collect = lambda weight: collect_rows(weight, dp_size)

    qkv_ctrl = collect(w_qkv_ctrl)
    ctrl = collect(jnp.concatenate([w_out_ctrl, w_join], axis=1))
    columns = w_qkv_space.reshape(-1, 3, view_size, width // view_size)
    columns = lax.dynamic_index_in_dim(columns, view, 2, keepdims=False)
    space = collect(jnp.concatenate([w_out_space, columns.reshape(-1, 3 * width // view_size)], axis=1))
    time = collect(jnp.concatenate([w_qkv_time, w_out_time], axis=1))

    base = latent.reshape(tokens, width).astype(jnp.float32)
    ctrl_in = base + condition.reshape(tokens, width).astype(jnp.float32)
    packed = project(modulate(ctrl_in, mod_ctrl), qkv_ctrl)
    parts = heads_of(packed, qk_gain[0], HEADS)
    by_frame = [part.reshape(HEADS * frames_here, patches, head_size) for part in parts]
    attended = attend(*by_frame, None).reshape(HEADS, tokens, head_size)
    flat = attended.transpose(1, 0, 2).reshape(tokens, width)
    control = (ctrl_in + mod_ctrl[2] * project(flat, ctrl, 0, width)).astype(jnp.bfloat16)
    joined = base + project(control, ctrl, width, width)

    normed = modulate(joined, mod_space)
    upward, downward = [normed], [normed]
    for _ in range(view_size - 1):
        upward.append(lax.ppermute(upward[-1], "view", [(i, i + 1) for i in range(view_size - 1)]))
        downward.append(lax.ppermute(downward[-1], "view", [(i + 1, i) for i in range(view_size - 1)]))
    everyone = [normed] + [jnp.where(view >= t, upward[t], downward[view_size - t]) for t in range(1, view_size)]
    cameras = (view - jnp.arange(view_size)) % view_size
    everyone = jnp.stack(everyone).reshape(view_size * tokens, width)
    packed = project(everyone, space[:, width:])
    parts = heads_of(packed, qk_gain[1], view_heads)
    by_frame = [
        part.reshape(view_heads, view_size, frames_here, patches, head_size)
        .transpose(0, 2, 1, 3, 4)
        .reshape(view_heads * frames_here, view_size * patches, head_size)
        for part in parts
    ]
    near = camera_mask(cycle_order)[cameras][:, cameras]
    near = jnp.repeat(jnp.repeat(near, patches, 0), patches, 1)
    attended = attend(*by_frame, near).reshape(view_heads, frames_here, view_size, patches, head_size)
    attended = attended.transpose(2, 1, 3, 0, 4).reshape(view_size, tokens, width // view_size)
    attended = lax.all_to_all(attended[cameras], "view", split_axis=0, concat_axis=0, tiled=True)
    flat = attended.transpose(1, 0, 2).reshape(tokens, width)
    spaced = (joined + mod_space[2] * project(flat, space, 0, width)).astype(jnp.bfloat16)

    spaced = spaced.reshape(1, frames_here, patches, width)
    patched = lax.all_to_all(spaced, "seq", split_axis=2, concat_axis=1, tiled=True)
    frames, patch_here = patched.shape[1:3]
    stream = patched.reshape(frames * patch_here, width).astype(jnp.float32)
    packed = project(modulate(stream, mod_time), time, 0, 3 * width)
    parts = heads_of(packed, qk_gain[2], HEADS)
    own_live = lax.dynamic_index_in_dim(live_frames, view, 0, keepdims=False)
    place = jnp.arange(frames * patch_here, dtype=jnp.int32)
    same = place[:, None] % patch_here == place[None, :] % patch_here
    alive = place[None, :] // patch_here < own_live
    attended = attend(*parts, same & alive)
    flat = attended.transpose(1, 0, 2).reshape(frames * patch_here, width)
    result = stream + mod_time[2] * project(flat, time, 3 * width, width)
    return result.astype(jnp.bfloat16).reshape(patched.shape)


def solution(mesh):
    placed = (
        P(("dp", "view"), "seq", None, None),
        P(("dp", "view"), "seq", None, None),
        P("dp"),
        P("dp"),
        P("seq", None),
        P("seq", None),
        P("seq", None),
        P("seq", None),
        P("seq", None),
        P("seq", None),
        P("seq", None),
        P("dp", None),
        P("dp", None),
        P("dp", None),
        P(),
    )
    sizes = mesh.shape["view"], mesh.shape["dp"]

    def run(*arrays):
        return per_device(*sizes, *arrays)

    return jax.shard_map(
        run,
        mesh=mesh,
        in_specs=placed,
        out_specs=P(("dp", "view"), None, "seq", None),
        check_vma=False,
    )
```
